768 devices in a mesh: grp: 2 (over x_hi), seq: 12 (over z), tp: 32 (over x_lo, y, core).
Axes of the slice: x: 4 (x_hi: 2, x_lo: 2; x = x_hi * 2 + x_lo), y: 8, z: 12, core: 2. Of those that a mesh axis runs over, the one named last changes fastest.
Arguments:
- queries: bfloat16 [2, 73728, 1792], P('grp', ('seq', 'tp')), may hold values from -40 to 40
- keys: bfloat16 [2, 73728, 256], P('grp', ('seq', 'tp')), may hold values from -40 to 40
- values: bfloat16 [2, 73728, 256], P('grp', ('seq', 'tp')), may hold values from -6 to 6
- grad_out: bfloat16 [2, 73728, 1792], P('grp', ('seq', 'tp')), may hold values from -6 to 6
- slot_pos: int32 [2, 73728], P('grp', ('seq', 'tp')), may hold values from -1 to 129023, as said below
- counts: int32 [2, 384], P('grp', ('seq', 'tp')), may hold values from 144 to 192, as said below
- seg_id: int32 [129024], P(('seq', 'tp')), may hold values from 0 to 306, as said below
Outputs:
- attended: bfloat16 [2, 73728, 1792], P('grp', ('seq', 'tp'))
- grad_queries: bfloat16 [2, 73728, 1792], P('grp', ('seq', 'tp'))
- key_gradients: bfloat16 [2, 73728, 256], P('grp', ('seq', 'tp'))
- value_gradients: bfloat16 [2, 73728, 256], P('grp', ('seq', 'tp'))
The draws below stay inside these ranges and needn't reach their ends.
Inputs may be any that keep to these rules, and one draw needn't show every extreme that they name: Each position block holds 336 positions, and its und and gen counts add up to 336; some block has exactly 192 understanding tokens and some other exactly 192 generation tokens. `slot_pos`: the live slots of a modality in block b hold, in increasing order, that modality's positions among b * 336 to (b + 1) * 336 - 1; every position is held by exactly one live slot; the slots after the live ones hold -1. `seg_id`: segment ids start at 0 and rise by one from segment to segment; a segment covers 1 to 673 consecutive positions, and one covers exactly 673; the number of segments is fixed by the sizes.
All inputs are finite; a program needn't handle non-finite values.
Results may differ from the reference program's by a relative error of at most 0.03.
Values may be sent and summed in bfloat16 or wider, within the bound.
No kernel may reach another device: no remote copies, remote signals or barrier semaphores. Data moves between devices by JAX's collectives and lax.ppermute only.
A program may use at most 64 MiB of HBM per device.

```python
import jax
import jax.numpy as jnp
from jax import lax

QUERY_HEADS = 14
KEY_HEADS = 2
HEAD_SIZE = 128
BLOCK_TOKENS = 192
KEY_BLOCK_SPAN = 3
QUERY_PER_KEY = 7
BLOCK = 336
BLOCK_COUNT = 384
MODALITY_SLOTS = 73728
LENGTH = 129024
SEGMAX = 673


def slot_tables(key):
    key = jax.random.fold_in(key, 101)
    key_count, key_perm = jax.random.split(key)
    under = jax.random.randint(key_count, (BLOCK_COUNT,), BLOCK - BLOCK_TOKENS, BLOCK_TOKENS + 1)
    under = under.at[0].set(BLOCK_TOKENS)
    under = under.at[BLOCK_COUNT - 1].set(BLOCK - BLOCK_TOKENS)
    perms = jax.vmap(lambda sub: jax.random.permutation(sub, BLOCK))(jax.random.split(key_perm, BLOCK_COUNT))
    places = jnp.arange(BLOCK, dtype=jnp.int32)
    score = jnp.where(perms < under[:, None], 0, BLOCK) + places[None, :]
    order = jnp.argsort(score, axis=1).astype(jnp.int32)
    slots = jnp.arange(BLOCK_TOKENS, dtype=jnp.int32)
    block_offset = (jnp.arange(BLOCK_COUNT, dtype=jnp.int32) * BLOCK)[:, None]
    und_take = jnp.take_along_axis(order, jnp.broadcast_to(slots[None, :], (BLOCK_COUNT, BLOCK_TOKENS)), 1)
    und_pos = jnp.where(slots[None, :] < under[:, None], und_take + block_offset, -1)
    gen_index = (under[:, None] + slots[None, :]) % BLOCK
    gen_take = jnp.take_along_axis(order, gen_index, 1)
    gen_pos = jnp.where(slots[None, :] < BLOCK - under[:, None], gen_take + block_offset, -1)
    positions = jnp.stack([und_pos, gen_pos]).reshape(2, BLOCK_COUNT * BLOCK_TOKENS).astype(jnp.int32)
    tallies = jnp.stack([under, BLOCK - under]).astype(jnp.int32)
    return (positions, tallies)


def draw_slot_pos(key, part):
    return slot_tables(key)[0]


def draw_counts(key, part):
    return slot_tables(key)[1]


def draw_seg_id(key, part):
    key = jax.random.fold_in(key, 5)
    lowest = BLOCK // 2 + 1
    period = SEGMAX + lowest
    whole_pairs = LENGTH // period
    remain = LENGTH % period
    number = whole_pairs + 1
    first = jax.random.randint(key, (number,), lowest, SEGMAX + 1).astype(jnp.int32)
    first = first.at[0].set(SEGMAX)
    first = first.at[whole_pairs].set(jnp.maximum(first[whole_pairs], min(remain, SEGMAX)))
    second = period - first
    lengths = jnp.stack([first, second], axis=1).reshape(2 * number)
    ends = jnp.cumsum(lengths)
    return jnp.searchsorted(ends, jnp.arange(LENGTH, dtype=jnp.int32), side='right').astype(jnp.int32)


def draw_keys(key, part):
    key = jax.random.fold_in(key, 13)
    array_shape = (2, MODALITY_SLOTS, KEY_HEADS * HEAD_SIZE)
    drawn = jax.random.truncated_normal(key, -6.0, 6.0, array_shape, jnp.float32)
    return drawn.astype(jnp.bfloat16)


def draw_queries(key, part):
    key = jax.random.fold_in(key, 17)
    array_shape = (2, MODALITY_SLOTS, QUERY_HEADS * HEAD_SIZE)
    drawn = jax.random.truncated_normal(key, -6.0, 6.0, array_shape, jnp.float32)
    return drawn.astype(jnp.bfloat16)


def steps_of(key, dims, cuts, least, high):
    def one(axis_at, shards_of):
        steps = jax.random.uniform(jax.random.fold_in(jax.random.fold_in(key, 6), axis_at), (shards_of,), jnp.float32, least / len(cuts), high / len(cuts))
        return jnp.repeat(jnp.exp(steps), dims[axis_at] // shards_of).reshape((-1,) + (1,) * (len(dims) - axis_at - 1))

    gain = one(*cuts[0])
    for cut in cuts[1:]:
        gain = gain * one(*cut)
    return gain


def normal_values(rng, extent, scale, bound, pieces=(), kind=jnp.bfloat16):
    array = scale * jax.random.normal(rng, extent, jnp.float32)
    if pieces:
        array = array * steps_of(rng, extent, pieces, -0.22, 0.18)
    return jnp.clip(array, -bound, bound).astype(kind)


def setup_inputs(seed: int = 0) -> dict:
    splits = jax.random.split(jax.random.key(seed), 8)
    return {
        "queries": draw_queries(jax.random.fold_in(splits[7], 71), 0),
        "keys": draw_keys(jax.random.fold_in(splits[7], 71), 0),
        "values": normal_values(splits[2], (2, MODALITY_SLOTS, KEY_HEADS * HEAD_SIZE), 1.0, 6.0, ((0, 2), (1, 384))),
        "grad_out": normal_values(splits[3], (2, MODALITY_SLOTS, QUERY_HEADS * HEAD_SIZE), 1.0, 6.0, ((0, 2), (1, 384))),
        "slot_pos": draw_slot_pos(jax.random.fold_in(splits[7], 71), 0),
        "counts": draw_counts(jax.random.fold_in(splits[7], 71), 0),
        "seg_id": draw_seg_id(jax.random.fold_in(splits[7], 71), 0),
    }


def head_forward(qh, kh, vh, mask, live, scale):
    scores = jnp.einsum("qgd,kd->gqk", qh.astype(jnp.float32), kh.astype(jnp.float32)) * scale
    scores = jnp.where(mask[None], scores, -jnp.inf)
    top = jnp.max(scores, axis=-1)
    top = jnp.where(live[None], top, 0.0)
    expo = jnp.exp(scores - top[..., None])
    total = jnp.sum(expo, axis=-1)
    total = jnp.where(live[None], total, 1.0)
    weights = (expo / total[..., None]).astype(jnp.bfloat16)
    result = jnp.einsum("gqk,kd->qgd", weights.astype(jnp.float32), vh.astype(jnp.float32))
    result = jnp.where(live[:, None, None], result, 0.0).astype(jnp.bfloat16)
    return result, top + jnp.log(total)


def head_backward(qh, kh, vh, oh, dh, mask, lse, scale):
    scores = jnp.einsum("qgd,kd->gqk", qh.astype(jnp.float32), kh.astype(jnp.float32)) * scale
    prob = jnp.exp(jnp.where(mask[None], scores - lse[..., None], -jnp.inf))
    delta = jnp.transpose(jnp.sum(oh.astype(jnp.float32) * dh.astype(jnp.float32), axis=-1))
    dprob = jnp.einsum("qgd,kd->gqk", dh.astype(jnp.float32), vh.astype(jnp.float32))
    dscore = (prob * (dprob - delta[..., None]) * scale).astype(jnp.bfloat16).astype(jnp.float32)
    grad_q = jnp.einsum("gqk,kd->qgd", dscore, kh.astype(jnp.float32))
    grad_k = jnp.einsum("gqk,qgd->kd", dscore, qh.astype(jnp.float32))
    grad_v = jnp.einsum("gqk,qgd->kd", prob.astype(jnp.bfloat16).astype(jnp.float32), dh.astype(jnp.float32))
    return grad_q, grad_k, grad_v


def reference(queries, keys, values, grad_out, slot_pos, counts, seg_id):
    scale = 1.0 / (HEAD_SIZE ** 0.5)
    padding_margin = KEY_BLOCK_SPAN - 1
    within = (jnp.arange(MODALITY_SLOTS, dtype=jnp.int32) % BLOCK_TOKENS)[None, :]
    live = within < jnp.repeat(counts, BLOCK_TOKENS, axis=1)
    seg = jnp.where(live, seg_id[jnp.clip(slot_pos, 0, LENGTH - 1)], -1).astype(jnp.int32)
    query_blocks = queries.reshape(2, BLOCK_COUNT, BLOCK_TOKENS, QUERY_HEADS * HEAD_SIZE)
    gradient_blocks = grad_out.reshape(2, BLOCK_COUNT, BLOCK_TOKENS, QUERY_HEADS * HEAD_SIZE)
    live_blocks = live.reshape(2, BLOCK_COUNT, BLOCK_TOKENS)
    pos_blocks = slot_pos.reshape(2, BLOCK_COUNT, BLOCK_TOKENS)
    seg_blocks = seg.reshape(2, BLOCK_COUNT, BLOCK_TOKENS)
    padded_key_value = jnp.zeros((2, padding_margin, BLOCK_TOKENS, KEY_HEADS * HEAD_SIZE), jnp.bfloat16)
    padded_keys = jnp.concatenate([padded_key_value, keys.reshape(2, BLOCK_COUNT, BLOCK_TOKENS, KEY_HEADS * HEAD_SIZE)], 1)
    padded_values = jnp.concatenate([padded_key_value, values.reshape(2, BLOCK_COUNT, BLOCK_TOKENS, KEY_HEADS * HEAD_SIZE)], 1)
    pos_pad = jnp.concatenate([jnp.zeros((2, padding_margin, BLOCK_TOKENS), jnp.int32), pos_blocks], 1)
    seg_pad = jnp.concatenate([jnp.full((2, padding_margin, BLOCK_TOKENS), -1, jnp.int32), seg_blocks], 1)
    token_rows = 2 * BLOCK_TOKENS
    window_width = 2 * KEY_BLOCK_SPAN * BLOCK_TOKENS

    def step(carry, block_index):
        key_gradient_total, value_gradient_total = carry
        query_block = lax.dynamic_index_in_dim(query_blocks, block_index, 1, keepdims=False).reshape(token_rows, KEY_HEADS, QUERY_PER_KEY, HEAD_SIZE)
        gradient_block = lax.dynamic_index_in_dim(gradient_blocks, block_index, 1, keepdims=False).reshape(token_rows, KEY_HEADS, QUERY_PER_KEY, HEAD_SIZE)
        lb = lax.dynamic_index_in_dim(live_blocks, block_index, 1, keepdims=False).reshape(token_rows)
        pb = lax.dynamic_index_in_dim(pos_blocks, block_index, 1, keepdims=False).reshape(token_rows)
        sb = lax.dynamic_index_in_dim(seg_blocks, block_index, 1, keepdims=False).reshape(token_rows)
        key_window_rows = lax.dynamic_slice_in_dim(padded_keys, block_index, KEY_BLOCK_SPAN, 1).reshape(window_width, KEY_HEADS * HEAD_SIZE)
        value_window_rows = lax.dynamic_slice_in_dim(padded_values, block_index, KEY_BLOCK_SPAN, 1).reshape(window_width, KEY_HEADS * HEAD_SIZE)
        pw = lax.dynamic_slice_in_dim(pos_pad, block_index, KEY_BLOCK_SPAN, 1).reshape(window_width)
        sw = lax.dynamic_slice_in_dim(seg_pad, block_index, KEY_BLOCK_SPAN, 1).reshape(window_width)
        mask = lb[:, None] & (sw[None, :] == sb[:, None]) & (sw[None, :] >= 0) & (pw[None, :] <= pb[:, None])
        out_heads, dq_heads, key_gradient_heads, value_gradient_heads = [], [], [], []
        for head_number in range(KEY_HEADS):
            kh = key_window_rows[:, head_number * HEAD_SIZE:(head_number + 1) * HEAD_SIZE]
            vh = value_window_rows[:, head_number * HEAD_SIZE:(head_number + 1) * HEAD_SIZE]
            oh, lse = head_forward(query_block[:, head_number], kh, vh, mask, lb, scale)
            gq, gk, gv = head_backward(query_block[:, head_number], kh, vh, oh, gradient_block[:, head_number], mask, lse, scale)
            out_heads.append(oh)
            dq_heads.append(gq.astype(jnp.bfloat16))
            key_gradient_heads.append(gk)
            value_gradient_heads.append(gv)
        out_b = jnp.stack(out_heads, axis=1).reshape(token_rows, QUERY_HEADS * HEAD_SIZE)
        dq_b = jnp.stack(dq_heads, axis=1).reshape(token_rows, QUERY_HEADS * HEAD_SIZE)
        key_gradient_extra = jnp.concatenate(key_gradient_heads, axis=1).reshape(2, KEY_BLOCK_SPAN, BLOCK_TOKENS, KEY_HEADS * HEAD_SIZE)
        value_gradient_extra = jnp.concatenate(value_gradient_heads, axis=1).reshape(2, KEY_BLOCK_SPAN, BLOCK_TOKENS, KEY_HEADS * HEAD_SIZE)
        key_gradient_total = lax.dynamic_update_slice_in_dim(key_gradient_total, lax.dynamic_slice_in_dim(key_gradient_total, block_index, KEY_BLOCK_SPAN, 1) + key_gradient_extra, block_index, 1)
        value_gradient_total = lax.dynamic_update_slice_in_dim(value_gradient_total, lax.dynamic_slice_in_dim(value_gradient_total, block_index, KEY_BLOCK_SPAN, 1) + value_gradient_extra, block_index, 1)
        return (key_gradient_total, value_gradient_total), (out_b, dq_b)

    window_start = jnp.zeros((2, BLOCK_COUNT + padding_margin, BLOCK_TOKENS, KEY_HEADS * HEAD_SIZE), jnp.float32)
    (key_gradient_total, value_gradient_total), (out_all, dq_all) = lax.scan(step, (window_start, window_start), jnp.arange(BLOCK_COUNT, dtype=jnp.int32))
    attended = jnp.transpose(out_all.reshape(BLOCK_COUNT, 2, BLOCK_TOKENS, QUERY_HEADS * HEAD_SIZE), (1, 0, 2, 3)).reshape(2, MODALITY_SLOTS, QUERY_HEADS * HEAD_SIZE)
    grad_queries = jnp.transpose(dq_all.reshape(BLOCK_COUNT, 2, BLOCK_TOKENS, QUERY_HEADS * HEAD_SIZE), (1, 0, 2, 3)).reshape(2, MODALITY_SLOTS, QUERY_HEADS * HEAD_SIZE)
    key_gradients = key_gradient_total[:, padding_margin:].reshape(2, MODALITY_SLOTS, KEY_HEADS * HEAD_SIZE).astype(jnp.bfloat16)
    value_gradients = value_gradient_total[:, padding_margin:].reshape(2, MODALITY_SLOTS, KEY_HEADS * HEAD_SIZE).astype(jnp.bfloat16)
    return (attended, grad_queries, key_gradients, value_gradients)
```

```python
import jax
import jax.numpy as jnp
from jax import lax
from jax.experimental import pallas as pl
from jax.experimental.pallas import tpu as pltpu
from jax.sharding import PartitionSpec as P

TOKENS = 192
HEAD = 128
SHARING = 7
KEY_HEADS = 2
BLOCK = 336
PIECES = 6
WINDOW = PIECES * TOKENS
META = 16
ROWS = TOKENS + META
KV = 2 * KEY_HEADS * HEAD
F32 = jnp.float32
BF16 = jnp.bfloat16
SCALE = HEAD**-0.5
LOG2E = 1.4426950408889634
VMEM = pl.BlockSpec(memory_space=pltpu.VMEM)
SMEM = pl.BlockSpec(memory_space=pltpu.SMEM)


def dot(a, b, contract):
    return lax.dot_general(a, b, (contract, ((), ())), preferred_element_type=F32)


def nt(a, b):
    return dot(a, b, ((1,), (1,)))


def nn(a, b):
    return dot(a, b, ((1,), (0,)))


def tn(a, b):
    return dot(a, b, ((0,), (0,)))


def pack_kernel(keys, values, slot_pos, counts, seg_id, packed):
    half = KEY_HEADS * HEAD
    packed[0:TOKENS, 0:half] = keys[0]
    packed[0:TOKENS, half:KV] = values[0]
    pos = slot_pos[...].astype(F32)
    local = pos - jnp.floor((pos + 0.5) * (1.0 / BLOCK)) * BLOCK
    local = local.astype(jnp.int32)
    live = lax.broadcasted_iota(jnp.int32, (1, TOKENS), 1) < counts[0, 0]
    place = lax.broadcasted_iota(jnp.int32, (BLOCK, TOKENS), 0)
    onehot = jnp.where((place == local) & live, 1.0, 0.0).astype(BF16)
    seg = seg_id[...] + 1
    digit = lax.broadcasted_iota(jnp.int32, (META, BLOCK), 0)
    low = (seg & 255).astype(F32)
    high = (seg >> 8).astype(F32)
    digits = jnp.where(digit == 2, low, jnp.where(digit == 3, high, 0.0))
    facts = nn(digits.astype(BF16), onehot)
    row = lax.broadcasted_iota(jnp.int32, (META, TOKENS), 0)
    live_pos = jnp.where(live, local, 0)
    facts = jnp.where(row == 0, (live_pos & 255).astype(F32), facts)
    facts = jnp.where(row == 1, (live_pos >> 8).astype(F32), facts)
    packed[TOKENS:ROWS, :] = jnp.zeros((META, KV), BF16)
    packed[TOKENS:ROWS, 0:TOKENS] = facts.astype(BF16)


def pack(keys, values, slot_pos, counts, seg_id):
    return pl.pallas_call(
        pack_kernel,
        out_shape=jax.ShapeDtypeStruct((ROWS, KV), BF16),
        in_specs=[VMEM, VMEM, VMEM, SMEM, VMEM],
        out_specs=VMEM,
    )(keys, values, slot_pos, counts, seg_id)


def fill_bias(pieces, bias):
    eye = lax.broadcasted_iota(jnp.int32, (TOKENS, TOKENS), 0) == lax.broadcasted_iota(jnp.int32, (TOKENS, TOKENS), 1)
    columns = nt(eye.astype(BF16), pieces[0][TOKENS:ROWS, 0:TOKENS])
    query_pos = columns[:, 0:1] + columns[:, 1:2] * 256.0
    query_seg = columns[:, 2:3] + columns[:, 3:4] * 256.0
    live = query_seg > 0.5
    wanted = jnp.where(live, query_seg, -1.0)
    for at in range(PIECES):
        facts = pieces[at][TOKENS:ROWS, 0:TOKENS].astype(F32)
        visible = facts[2:3] + facts[3:4] * 256.0 == wanted
        if at < 2:
            visible = visible & (facts[0:1] + facts[1:2] * 256.0 <= query_pos)
        bias[:, at * TOKENS : (at + 1) * TOKENS] = jnp.where(visible, 0.0, -1e30)
    return live


def attention_kernel(queries, grads, *refs):
    pieces = refs[:PIECES]
    attended, grad_queries = refs[PIECES : PIECES + 2]
    returned = refs[PIECES + 2 : 2 * PIECES + 2]
    keys, values, bias, grad_keys, grad_values = refs[2 * PIECES + 2 :]
    for at in range(PIECES):
        for h in range(KEY_HEADS):
            span = pl.ds(at * TOKENS, TOKENS)
            keys[h, span, :] = pieces[at][0:TOKENS, h * HEAD : (h + 1) * HEAD]
            values[h, span, :] = pieces[at][0:TOKENS, (KEY_HEADS + h) * HEAD : (KEY_HEADS + h + 1) * HEAD]
    live = fill_bias(pieces, bias)
    for g in range(SHARING):
        for h in range(KEY_HEADS):
            column = pl.ds((h * SHARING + g) * HEAD, HEAD)
            key, value = keys[h], values[h]
            query, grad = queries[0, :, column], grads[0, :, column]
            scores = nt(query, key) * (SCALE * LOG2E) + bias[...]
            top = jnp.max(scores, axis=1, keepdims=True)
            expo = jnp.exp2(scores - top)
            total = jnp.sum(expo, axis=1, keepdims=True)
            prob = expo * jnp.where(live, 1.0 / total, 0.0)
            prob_b = prob.astype(BF16)
            result = nn(prob_b, value).astype(BF16)
            attended[0, :, column] = result
            delta = jnp.sum(result.astype(F32) * grad.astype(F32), axis=1, keepdims=True)
            dscore = (prob * (nt(grad, value) - delta)).astype(BF16)
            grad_queries[0, :, column] = (nn(dscore, key) * SCALE).astype(BF16)
            grad_value = tn(grad, prob_b)
            grad_key = tn(query, dscore)
            if g == 0:
                grad_values[h] = grad_value
                grad_keys[h] = grad_key
            else:
                grad_values[h] += grad_value
                grad_keys[h] += grad_key
    for h in range(KEY_HEADS):
        grad_key = grad_keys[h].T * SCALE
        grad_value = grad_values[h].T
        for at in range(PIECES):
            span = slice(at * TOKENS, (at + 1) * TOKENS)
            returned[at][:, h * HEAD : (h + 1) * HEAD] = grad_key[span].astype(BF16)
            returned[at][:, (KEY_HEADS + h) * HEAD : (KEY_HEADS + h + 1) * HEAD] = grad_value[span].astype(BF16)


def attention(queries, grads, pieces):
    wide = jax.ShapeDtypeStruct(queries.shape, BF16)
    return pl.pallas_call(
        attention_kernel,
        out_shape=[wide, wide] + [jax.ShapeDtypeStruct((TOKENS, KV), BF16)] * PIECES,
        in_specs=[VMEM] * (2 + PIECES),
        out_specs=[VMEM] * (2 + PIECES),
        scratch_shapes=[
            pltpu.VMEM((KEY_HEADS, WINDOW, HEAD), BF16),
            pltpu.VMEM((KEY_HEADS, WINDOW, HEAD), BF16),
            pltpu.VMEM((TOKENS, WINDOW), F32),
            pltpu.VMEM((KEY_HEADS, HEAD, WINDOW), F32),
            pltpu.VMEM((KEY_HEADS, HEAD, WINDOW), F32),
        ],
        compiler_params=pltpu.CompilerParams(vmem_limit_bytes=48 * 2**20),
        cost_estimate=pl.CostEstimate(flops=4_800_000_000, bytes_accessed=6_000_000, transcendentals=3_100_000),
    )(queries, grads, *pieces)


BLOCKS = ("seq", "tp")
ALL = ("grp", "seq", "tp")


def shift_blocks(array, distance):
    count = lax.axis_size(BLOCKS)
    route = [(i, i + distance) for i in range(count) if 0 <= i + distance < count]
    return lax.ppermute(array, BLOCKS, route)


def shift_across(array, distance):
    count = lax.axis_size(BLOCKS)
    route = [
        (g * count + i, (1 - g) * count + i + distance)
        for g in range(2)
        for i in range(count)
        if 0 <= i + distance < count
    ]
    return lax.ppermute(array, ALL, route)


def exchange(array):
    return lax.ppermute(array, "grp", [(0, 1), (1, 0)])


def swap_cores(array):
    count = lax.axis_size(BLOCKS)
    return lax.ppermute(array, BLOCKS, [(i, i ^ 1) for i in range(count)])


def body(queries, keys, values, grad_out, slot_pos, counts, seg_id):
    core = lax.axis_index(BLOCKS) % 2
    own = pack(keys, values, slot_pos, counts, seg_id.reshape(1, BLOCK))
    behind = shift_blocks(own, 2)
    other = exchange(own)
    across = shift_across(own, 2)
    first = jnp.where(core == 0, jnp.stack([own, other]), jnp.stack([behind, across]))
    swapped = swap_cores(first)
    pieces = (own, other, swapped[0], swapped[1], behind, across)
    attended, grad_queries, *parts = attention(queries, grad_out, pieces)
    back = swap_cores(jnp.stack([parts[2], parts[3]])).astype(F32)
    near = jnp.where(core == 0, back, 0.0)
    far = jnp.where(core == 0, 0.0, back)
    from_ahead = shift_blocks((parts[4].astype(F32) + far[0]).astype(BF16), -2)
    from_across = shift_across((parts[5].astype(F32) + far[1]).astype(BF16), -2)
    from_other = exchange((parts[1].astype(F32) + near[1]).astype(BF16))
    total = parts[0].astype(F32) + near[0] + from_ahead.astype(F32) + from_across.astype(F32) + from_other.astype(F32)
    total = total.astype(BF16)
    half = KEY_HEADS * HEAD
    return attended, grad_queries, total[None, :, :half], total[None, :, half:]


def solution(mesh):
    rows = P("grp", BLOCKS, None)
    slots = P("grp", BLOCKS)
    return jax.shard_map(
        body,
        mesh=mesh,
        in_specs=(rows, rows, rows, rows, slots, slots, P(BLOCKS)),
        out_specs=(rows, rows, rows, rows),
        check_vma=False,
    )
```

```python
import jax
import jax.numpy as jnp
from jax import lax
from jax.experimental import pallas as pl
from jax.experimental.pallas import tpu as pltpu
from jax.sharding import PartitionSpec as P

TOKENS = 192
HEAD = 128
SHARING = 7
KEY_HEADS = 2
BLOCK = 336
PIECES = 6
WINDOW = PIECES * TOKENS
NEAR = 2 * TOKENS
META = 16
ROWS = TOKENS + META
KV = 2 * KEY_HEADS * HEAD
F32 = jnp.float32
BF16 = jnp.bfloat16
SCALE = HEAD**-0.5
LOG2E = 1.4426950408889634
VMEM = pl.BlockSpec(memory_space=pltpu.VMEM)


def dot(a, b, contract):
    return lax.dot_general(a, b, (contract, ((), ())), preferred_element_type=F32)


def nt(a, b):
    return dot(a, b, ((1,), (1,)))


def nn(a, b):
    return dot(a, b, ((1,), (0,)))


def pack_kernel(keys, values, slot_pos, counts, seg_id, packed):
    half = KEY_HEADS * HEAD
    packed[0:TOKENS, 0:half] = keys[0]
    packed[0:TOKENS, half:KV] = values[0]
    pos = slot_pos[...].astype(F32)
    local = pos - jnp.floor((pos + 0.5) * (1.0 / BLOCK)) * BLOCK
    local = local.astype(jnp.int32)
    live = lax.broadcasted_iota(jnp.int32, (1, TOKENS), 1) < counts[...]
    place = lax.broadcasted_iota(jnp.int32, (BLOCK, TOKENS), 0)
    onehot = jnp.where((place == local) & live, 1.0, 0.0).astype(BF16)
    seg = seg_id[...].reshape(1, BLOCK) + 1
    digit = lax.broadcasted_iota(jnp.int32, (META, BLOCK), 0)
    low = (seg & 255).astype(F32)
    high = (seg >> 8).astype(F32)
    digits = jnp.where(digit == 2, low, jnp.where(digit == 3, high, 0.0))
    facts = nn(digits.astype(BF16), onehot)
    row = lax.broadcasted_iota(jnp.int32, (META, TOKENS), 0)
    live_pos = jnp.where(live, local, 0)
    facts = jnp.where(row == 0, (live_pos & 255).astype(F32), facts)
    facts = jnp.where(row == 1, (live_pos >> 8).astype(F32), facts)
    packed[TOKENS:ROWS, :] = jnp.zeros((META, KV), BF16)
    packed[TOKENS:ROWS, 0:TOKENS] = facts.astype(BF16)


def pack(keys, values, slot_pos, counts, seg_id):
    return pl.pallas_call(
        pack_kernel,
        out_shape=jax.ShapeDtypeStruct((ROWS, KV), BF16),
        in_specs=[VMEM] * 5,
        out_specs=VMEM,
    )(keys, values, slot_pos, counts, seg_id)


def fill_bias(pieces, bias):
    eye = lax.broadcasted_iota(jnp.int32, (TOKENS, TOKENS), 0) == lax.broadcasted_iota(jnp.int32, (TOKENS, TOKENS), 1)
    columns = nt(eye.astype(BF16), pieces[0][TOKENS:ROWS, 0:TOKENS])
    query_pos = columns[:, 0:1] + columns[:, 1:2] * 256.0
    query_seg = columns[:, 2:3] + columns[:, 3:4] * 256.0
    live = query_seg > 0.5
    wanted = jnp.where(live, query_seg, -1.0)
    for at in range(PIECES):
        facts = pieces[at][TOKENS:ROWS, 0:TOKENS].astype(F32)
        visible = facts[2:3] + facts[3:4] * 256.0 == wanted
        if at < 2:
            visible = visible & (facts[0:1] + facts[1:2] * 256.0 <= query_pos)
        bias[:, at * TOKENS : (at + 1) * TOKENS] = jnp.where(visible, 0.0, -1e30)
    return live


def column(n):
    return pl.ds(n * HEAD, HEAD)


def staged(stages, offsets):
    order = [(g, h) for g in range(SHARING) for h in range(KEY_HEADS)]
    for step in range(len(order) + max(offsets)):
        for stage, offset in zip(stages, offsets):
            if 0 <= step - offset < len(order):
                stage(*order[step - offset])


def accumulate(total, h, first, term):
    if first:
        total[h] = term
    else:
        total[h] += term


def turn_kernel(queries, grads, packed, after, queries_here, grads_here, queries_t, grads_t, own):
    queries_here[...] = queries[0]
    grads_here[...] = grads[0]
    own[...] = packed[...]
    for n in range(SHARING * KEY_HEADS):
        queries_t[n] = queries[0, :, column(n)].T
        grads_t[n] = grads[0, :, column(n)].T


def turn(queries, grads, packed, after):
    heads = SHARING * KEY_HEADS
    wide = jax.ShapeDtypeStruct((TOKENS, heads * HEAD), BF16)
    turned = jax.ShapeDtypeStruct((heads, HEAD, TOKENS), BF16)
    return pl.pallas_call(
        turn_kernel,
        out_shape=[wide, wide, turned, turned, jax.ShapeDtypeStruct(packed.shape, BF16)],
        in_specs=[VMEM, VMEM, VMEM, pl.BlockSpec(memory_space=pl.ANY)],
        out_specs=[VMEM] * 5,
        compiler_params=pltpu.CompilerParams(vmem_limit_bytes=16 * 2**20),
        cost_estimate=pl.CostEstimate(flops=0, bytes_accessed=8_000_000, transcendentals=0),
    )(queries, grads, packed, after)


def attention_kernel(queries, grads, queries_t, grads_t, *refs):
    pieces = refs[:PIECES]
    attended, dscores, near_probs, middle, far, keys = refs[PIECES : PIECES + 6]
    values, bias, grad_keys, grad_values = refs[PIECES + 6 :]
    for at in range(PIECES):
        for h in range(KEY_HEADS):
            span = pl.ds(at * TOKENS, TOKENS)
            keys[h, span, :] = pieces[at][0:TOKENS, h * HEAD : (h + 1) * HEAD]
            values[h, span, :] = pieces[at][0:TOKENS, (KEY_HEADS + h) * HEAD : (KEY_HEADS + h + 1) * HEAD]
    live = fill_bias(pieces, bias)
    held = {}

    def products(g, h):
        at = column(h * SHARING + g)
        held[g, h] = nt(queries[:, at], keys[h]), nt(grads[:, at], values[h])

    def softmax(g, h):
        n = h * SHARING + g
        scores, dprob = held[g, h]
        grad = grads[:, column(n)]
        scores = scores * (SCALE * LOG2E) + bias[...]
        top = jnp.max(scores, axis=1, keepdims=True)
        expo = jnp.exp2(scores - top)
        total = jnp.sum(expo, axis=1, keepdims=True)
        prob = expo * jnp.where(live, 1.0 / total, 0.0)
        prob_b = prob.astype(BF16)
        result = nn(prob_b, values[h]).astype(BF16)
        attended[0, :, column(n)] = result
        delta = jnp.sum(result.astype(F32) * grad.astype(F32), axis=1, keepdims=True)
        dscore = (prob * (dprob - delta)).astype(BF16)
        dscores[n] = dscore
        near_probs[n] = prob_b[:, :NEAR]
        held[g, h] = prob_b[:, NEAR:], dscore[:, NEAR:]

    def sums(g, h):
        prob_b, dscore = held.pop((g, h))
        n = h * SHARING + g
        accumulate(grad_values, h, g == 0, nn(grads_t[n], prob_b))
        accumulate(grad_keys, h, g == 0, nn(queries_t[n], dscore))

    staged((products, softmax, sums), (0, 2, 3))
    for h in range(KEY_HEADS):
        grad_key = grad_keys[h].T * SCALE
        grad_value = grad_values[h].T
        for at in range(2):
            span = slice(at * TOKENS, (at + 1) * TOKENS)
            middle[at, :, column(h)] = grad_key[span].astype(BF16)
            middle[at, :, column(KEY_HEADS + h)] = grad_value[span].astype(BF16)
            span = slice((at + 2) * TOKENS, (at + 3) * TOKENS)
            far[at, :, column(h)] = grad_key[span]
            far[at, :, column(KEY_HEADS + h)] = grad_value[span]


def attention(queries, grads, queries_t, grads_t, pieces):
    heads = SHARING * KEY_HEADS
    return pl.pallas_call(
        attention_kernel,
        out_shape=[
            jax.ShapeDtypeStruct((1, TOKENS, heads * HEAD), BF16),
            jax.ShapeDtypeStruct((heads, TOKENS, WINDOW), BF16),
            jax.ShapeDtypeStruct((heads, TOKENS, NEAR), BF16),
            jax.ShapeDtypeStruct((2, TOKENS, KV), BF16),
            jax.ShapeDtypeStruct((2, TOKENS, KV), F32),
            jax.ShapeDtypeStruct((KEY_HEADS, WINDOW, HEAD), BF16),
        ],
        in_specs=[VMEM] * (4 + PIECES),
        out_specs=[VMEM] * 6,
        scratch_shapes=[
            pltpu.VMEM((KEY_HEADS, WINDOW, HEAD), BF16),
            pltpu.VMEM((TOKENS, WINDOW), F32),
            pltpu.VMEM((KEY_HEADS, HEAD, WINDOW - NEAR), F32),
            pltpu.VMEM((KEY_HEADS, HEAD, WINDOW - NEAR), F32),
        ],
        compiler_params=pltpu.CompilerParams(vmem_limit_bytes=32 * 2**20),
        cost_estimate=pl.CostEstimate(flops=3_500_000_000, bytes_accessed=12_000_000, transcendentals=3_100_000),
    )(queries, grads, queries_t, grads_t, *pieces)


def near_kernel(queries_t, grads_t, dscores, probs, near, grad_keys, grad_values):
    def sums(g, h):
        n = h * SHARING + g
        accumulate(grad_values, h, g == 0, nn(grads_t[n], probs[n]))
        accumulate(grad_keys, h, g == 0, nn(queries_t[n], dscores[n, :, :NEAR]))

    staged((sums,), (0,))
    for h in range(KEY_HEADS):
        grad_key = grad_keys[h].T * SCALE
        grad_value = grad_values[h].T
        for at in range(2):
            span = slice(at * TOKENS, (at + 1) * TOKENS)
            near[at, :, column(h)] = grad_key[span]
            near[at, :, column(KEY_HEADS + h)] = grad_value[span]


def near_gradients(queries_t, grads_t, dscores, probs):
    return pl.pallas_call(
        near_kernel,
        out_shape=jax.ShapeDtypeStruct((2, TOKENS, KV), F32),
        in_specs=[VMEM] * 4,
        out_specs=VMEM,
        scratch_shapes=[
            pltpu.VMEM((KEY_HEADS, HEAD, NEAR), F32),
            pltpu.VMEM((KEY_HEADS, HEAD, NEAR), F32),
        ],
        compiler_params=pltpu.CompilerParams(vmem_limit_bytes=24 * 2**20),
        cost_estimate=pl.CostEstimate(flops=530_000_000, bytes_accessed=6_000_000, transcendentals=0),
    )(queries_t, grads_t, dscores, probs)


def query_kernel(dscores, keys, grad_queries):
    for n in range(SHARING * KEY_HEADS):
        grad_queries[0, :, column(n)] = (nn(dscores[n], keys[n // SHARING]) * SCALE).astype(BF16)


def query_gradients(dscores, keys):
    return pl.pallas_call(
        query_kernel,
        out_shape=jax.ShapeDtypeStruct((1, TOKENS, SHARING * KEY_HEADS * HEAD), BF16),
        in_specs=[VMEM] * 2,
        out_specs=VMEM,
        compiler_params=pltpu.CompilerParams(vmem_limit_bytes=24 * 2**20),
        cost_estimate=pl.CostEstimate(flops=800_000_000, bytes_accessed=8_000_000, transcendentals=0),
    )(dscores, keys)


BLOCKS = ("seq", "tp")
ALL = ("grp", "seq", "tp")


def shift_blocks(array, distance):
    count = lax.axis_size(BLOCKS)
    route = [(i, i + distance) for i in range(count) if 0 <= i + distance < count]
    return lax.ppermute(array, BLOCKS, route)


def shift_across(array, distance):
    count = lax.axis_size(BLOCKS)
    route = [
        (g * count + i, (1 - g) * count + i + distance)
        for g in range(2)
        for i in range(count)
        if 0 <= i + distance < count
    ]
    return lax.ppermute(array, ALL, route)


def exchange(array):
    return lax.ppermute(array, "grp", [(0, 1), (1, 0)])


def swap_cores(array):
    count = lax.axis_size(BLOCKS)
    return lax.ppermute(array, BLOCKS, [(i, i ^ 1) for i in range(count)])


def body(queries, keys, values, grad_out, slot_pos, counts, seg_id):
    core = lax.axis_index(BLOCKS) % 2
    packed = pack(keys, values, slot_pos, counts, seg_id)
    other = exchange(packed)
    behind = shift_blocks(packed, 2)
    across = shift_blocks(other, 2)
    *turned, own = turn(queries, grad_out, packed, behind)
    early = swap_cores(jnp.where(core == 0, own, behind))
    late = swap_cores(jnp.where(core == 0, other, across))
    pieces = (own, other, early, late, behind, across)
    attended, dscores, near_probs, middle, far, keys = attention(*turned, pieces)
    back = swap_cores(middle)
    near = near_gradients(turned[2], turned[3], dscores, near_probs)
    back = back.astype(F32)
    far = (far + jnp.where(core == 0, 0.0, back)).astype(BF16)
    near = near + jnp.where(core == 0, back, 0.0)
    far, dscores = lax.optimization_barrier((far, dscores))
    from_across = shift_across(far[1], -2)
    from_other = exchange(near[1].astype(BF16))
    from_ahead = shift_blocks(far[0], -2)
    grad_queries = query_gradients(dscores, keys)
    half = KEY_HEADS * HEAD
    totals = [
        (near[0][:, at] + from_across[:, at].astype(F32) + from_other[:, at].astype(F32) + from_ahead[:, at].astype(F32))
        .astype(BF16)[None]
        for at in (slice(0, half), slice(half, KV))
    ]
    return attended, grad_queries, totals[0], totals[1]


def solution(mesh):
    rows = P("grp", BLOCKS, None)
    slots = P("grp", BLOCKS)
    return jax.shard_map(
        body,
        mesh=mesh,
        in_specs=(rows, rows, rows, rows, slots, slots, P(BLOCKS)),
        out_specs=(rows, rows, rows, rows),
        check_vma=False,
    )
```

```python
import jax
import jax.numpy as jnp
from jax import lax
from jax.experimental import pallas as pl
from jax.experimental.pallas import tpu as pltpu
from jax.sharding import PartitionSpec as P

TOKENS = 192
HEAD = 128
SHARING = 7
KEY_HEADS = 2
BLOCK = 336
PIECES = 6
WINDOW = PIECES * TOKENS
NEAR = 2 * TOKENS
META = 16
ROWS = TOKENS + META
KV = 2 * KEY_HEADS * HEAD
F32 = jnp.float32
BF16 = jnp.bfloat16
SCALE = HEAD**-0.5
LOG2E = 1.4426950408889634
VMEM = pl.BlockSpec(memory_space=pltpu.VMEM)


def dot(a, b, contract):
    return lax.dot_general(a, b, (contract, ((), ())), preferred_element_type=F32)


def nt(a, b):
    return dot(a, b, ((1,), (1,)))


def nn(a, b):
    return dot(a, b, ((1,), (0,)))


def pack_kernel(keys, values, slot_pos, counts, seg_id, packed):
    half = KEY_HEADS * HEAD
    packed[0:TOKENS, 0:half] = keys[0]
    packed[0:TOKENS, half:KV] = values[0]
    pos = slot_pos[...].astype(F32)
    local = pos - jnp.floor((pos + 0.5) * (1.0 / BLOCK)) * BLOCK
    local = local.astype(jnp.int32)
    live = lax.broadcasted_iota(jnp.int32, (1, TOKENS), 1) < counts[...]
    place = lax.broadcasted_iota(jnp.int32, (BLOCK, TOKENS), 0)
    onehot = jnp.where((place == local) & live, 1.0, 0.0).astype(BF16)
    seg = seg_id[...].reshape(1, BLOCK) + 1
    digit = lax.broadcasted_iota(jnp.int32, (META, BLOCK), 0)
    low = (seg & 255).astype(F32)
    high = (seg >> 8).astype(F32)
    digits = jnp.where(digit == 2, low, jnp.where(digit == 3, high, 0.0))
    facts = nn(digits.astype(BF16), onehot)
    row = lax.broadcasted_iota(jnp.int32, (META, TOKENS), 0)
    live_pos = jnp.where(live, local, 0)
    facts = jnp.where(row == 0, (live_pos & 255).astype(F32), facts)
    facts = jnp.where(row == 1, (live_pos >> 8).astype(F32), facts)
    packed[TOKENS:ROWS, :] = jnp.zeros((META, KV), BF16)
    packed[TOKENS:ROWS, 0:TOKENS] = facts.astype(BF16)


def pack(keys, values, slot_pos, counts, seg_id):
    return pl.pallas_call(
        pack_kernel,
        out_shape=jax.ShapeDtypeStruct((ROWS, KV), BF16),
        in_specs=[VMEM] * 5,
        out_specs=VMEM,
    )(keys, values, slot_pos, counts, seg_id)


def fill_bias(pieces, bias):
    eye = lax.broadcasted_iota(jnp.int32, (TOKENS, TOKENS), 0) == lax.broadcasted_iota(jnp.int32, (TOKENS, TOKENS), 1)
    columns = nt(eye.astype(BF16), pieces[0][TOKENS:ROWS, 0:TOKENS])
    query_pos = columns[:, 0:1] + columns[:, 1:2] * 256.0
    query_seg = columns[:, 2:3] + columns[:, 3:4] * 256.0
    live = query_seg > 0.5
    wanted = jnp.where(live, query_seg, -1.0)
    for at in range(PIECES):
        facts = pieces[at][TOKENS:ROWS, 0:TOKENS].astype(F32)
        visible = facts[2:3] + facts[3:4] * 256.0 == wanted
        if at < 2:
            visible = visible & (facts[0:1] + facts[1:2] * 256.0 <= query_pos)
        bias[:, at * TOKENS : (at + 1) * TOKENS] = jnp.where(visible, 0.0, -1e30)
    return live


def column(n):
    return pl.ds(n * HEAD, HEAD)


def staged(stages, offsets):
    order = [(g, h) for g in range(SHARING) for h in range(KEY_HEADS)]
    for step in range(len(order) + max(offsets)):
        for stage, offset in zip(stages, offsets):
            if 0 <= step - offset < len(order):
                stage(*order[step - offset])


def accumulate(total, h, first, term):
    if first:
        total[h] = term
    else:
        total[h] += term


def turn_kernel(queries, grads, packed, after, queries_here, grads_here, queries_t, grads_t, own):
    queries_here[...] = queries[0]
    grads_here[...] = grads[0]
    own[...] = packed[...]
    for n in range(SHARING * KEY_HEADS):
        queries_t[n] = queries[0, :, column(n)].T
        grads_t[n] = grads[0, :, column(n)].T


def turn(queries, grads, packed, after):
    heads = SHARING * KEY_HEADS
    wide = jax.ShapeDtypeStruct((TOKENS, heads * HEAD), BF16)
    turned = jax.ShapeDtypeStruct((heads, HEAD, TOKENS), BF16)
    return pl.pallas_call(
        turn_kernel,
        out_shape=[wide, wide, turned, turned, jax.ShapeDtypeStruct(packed.shape, BF16)],
        in_specs=[VMEM, VMEM, VMEM, pl.BlockSpec(memory_space=pl.ANY)],
        out_specs=[VMEM] * 5,
        compiler_params=pltpu.CompilerParams(vmem_limit_bytes=16 * 2**20),
        cost_estimate=pl.CostEstimate(flops=0, bytes_accessed=8_000_000, transcendentals=0),
    )(queries, grads, packed, after)


def attention_kernel(queries, grads, queries_t, grads_t, *refs):
    pieces = refs[:PIECES]
    attended, dscores, near_probs, middle, far, keys = refs[PIECES : PIECES + 6]
    values, bias, grad_keys, grad_values = refs[PIECES + 6 :]
    for at in range(PIECES):
        for h in range(KEY_HEADS):
            span = pl.ds(at * TOKENS, TOKENS)
            keys[h, span, :] = pieces[at][0:TOKENS, h * HEAD : (h + 1) * HEAD]
            values[h, span, :] = pieces[at][0:TOKENS, (KEY_HEADS + h) * HEAD : (KEY_HEADS + h + 1) * HEAD]
    live = fill_bias(pieces, bias)
    held = {}

    def products(g, h):
        at = column(h * SHARING + g)
        held[g, h] = nt(queries[:, at], keys[h]), nt(grads[:, at], values[h])

    def softmax(g, h):
        n = h * SHARING + g
        scores, dprob = held[g, h]
        grad = grads[:, column(n)]
        scores = scores * (SCALE * LOG2E) + bias[...]
        top = jnp.max(scores, axis=1, keepdims=True)
        expo = jnp.exp2(scores - top)
        total = jnp.sum(expo, axis=1, keepdims=True)
        prob = expo * jnp.where(live, 1.0 / total, 0.0)
        prob_b = prob.astype(BF16)
        result = nn(prob_b, values[h]).astype(BF16)
        attended[0, :, column(n)] = result
        delta = jnp.sum(result.astype(F32) * grad.astype(F32), axis=1, keepdims=True)
        dscore = (prob * (dprob - delta)).astype(BF16)
        dscores[n] = dscore
        near_probs[n] = prob_b[:, :NEAR]
        held[g, h] = prob_b[:, NEAR:], dscore[:, NEAR:]

    def sums(g, h):
        prob_b, dscore = held.pop((g, h))
        n = h * SHARING + g
        accumulate(grad_values, h, g == 0, nn(grads_t[n], prob_b))
        accumulate(grad_keys, h, g == 0, nn(queries_t[n], dscore))

    staged((products, softmax, sums), (0, 2, 3))
    for h in range(KEY_HEADS):
        grad_key = grad_keys[h].T * SCALE
        grad_value = grad_values[h].T
        for at in range(2):
            span = slice(at * TOKENS, (at + 1) * TOKENS)
            middle[at, :, column(h)] = grad_key[span].astype(BF16)
            middle[at, :, column(KEY_HEADS + h)] = grad_value[span].astype(BF16)
            span = slice((at + 2) * TOKENS, (at + 3) * TOKENS)
            far[at, :, column(h)] = grad_key[span]
            far[at, :, column(KEY_HEADS + h)] = grad_value[span]


def attention(queries, grads, queries_t, grads_t, pieces):
    heads = SHARING * KEY_HEADS
    return pl.pallas_call(
        attention_kernel,
        out_shape=[
            jax.ShapeDtypeStruct((1, TOKENS, heads * HEAD), BF16),
            jax.ShapeDtypeStruct((heads, TOKENS, WINDOW), BF16),
            jax.ShapeDtypeStruct((heads, TOKENS, NEAR), BF16),
            jax.ShapeDtypeStruct((2, TOKENS, KV), BF16),
            jax.ShapeDtypeStruct((2, TOKENS, KV), F32),
            jax.ShapeDtypeStruct((KEY_HEADS, WINDOW, HEAD), BF16),
        ],
        in_specs=[VMEM] * (4 + PIECES),
        out_specs=[VMEM] * 6,
        scratch_shapes=[
            pltpu.VMEM((KEY_HEADS, WINDOW, HEAD), BF16),
            pltpu.VMEM((TOKENS, WINDOW), F32),
            pltpu.VMEM((KEY_HEADS, HEAD, WINDOW - NEAR), F32),
            pltpu.VMEM((KEY_HEADS, HEAD, WINDOW - NEAR), F32),
        ],
        compiler_params=pltpu.CompilerParams(vmem_limit_bytes=32 * 2**20),
        cost_estimate=pl.CostEstimate(flops=3_500_000_000, bytes_accessed=12_000_000, transcendentals=3_100_000),
    )(queries, grads, queries_t, grads_t, *pieces)


def near_kernel(queries_t, grads_t, dscores, probs, near, grad_keys, grad_values):
    def sums(g, h):
        n = h * SHARING + g
        accumulate(grad_values, h, g == 0, nn(grads_t[n], probs[n]))
        accumulate(grad_keys, h, g == 0, nn(queries_t[n], dscores[n, :, :NEAR]))

    staged((sums,), (0,))
    for h in range(KEY_HEADS):
        grad_key = grad_keys[h].T * SCALE
        grad_value = grad_values[h].T
        for at in range(2):
            span = slice(at * TOKENS, (at + 1) * TOKENS)
            near[at, :, column(h)] = grad_key[span]
            near[at, :, column(KEY_HEADS + h)] = grad_value[span]


def near_gradients(queries_t, grads_t, dscores, probs):
    return pl.pallas_call(
        near_kernel,
        out_shape=jax.ShapeDtypeStruct((2, TOKENS, KV), F32),
        in_specs=[VMEM] * 4,
        out_specs=VMEM,
        scratch_shapes=[
            pltpu.VMEM((KEY_HEADS, HEAD, NEAR), F32),
            pltpu.VMEM((KEY_HEADS, HEAD, NEAR), F32),
        ],
        compiler_params=pltpu.CompilerParams(vmem_limit_bytes=24 * 2**20),
        cost_estimate=pl.CostEstimate(flops=530_000_000, bytes_accessed=6_000_000, transcendentals=0),
    )(queries_t, grads_t, dscores, probs)


def query_kernel(dscores, keys, attended, grad_queries, attended_out):
    attended_out[...] = attended[...]
    for n in range(SHARING * KEY_HEADS):
        grad_queries[0, :, column(n)] = (nn(dscores[n], keys[n // SHARING]) * SCALE).astype(BF16)


def query_gradients(dscores, keys, attended):
    return pl.pallas_call(
        query_kernel,
        out_shape=[jax.ShapeDtypeStruct((1, TOKENS, SHARING * KEY_HEADS * HEAD), BF16)] * 2,
        in_specs=[VMEM] * 3,
        out_specs=[VMEM] * 2,
        compiler_params=pltpu.CompilerParams(vmem_limit_bytes=24 * 2**20),
        cost_estimate=pl.CostEstimate(flops=800_000_000, bytes_accessed=8_000_000, transcendentals=0),
    )(dscores, keys, attended)


BLOCKS = ("seq", "tp")
ALL = ("grp", "seq", "tp")


def shift_blocks(array, distance):
    count = lax.axis_size(BLOCKS)
    route = [(i, i + distance) for i in range(count) if 0 <= i + distance < count]
    return lax.ppermute(array, BLOCKS, route)


def shift_across(array, distance):
    count = lax.axis_size(BLOCKS)
    route = [
        (g * count + i, (1 - g) * count + i + distance)
        for g in range(2)
        for i in range(count)
        if 0 <= i + distance < count
    ]
    return lax.ppermute(array, ALL, route)


def exchange(array):
    return lax.ppermute(array, "grp", [(0, 1), (1, 0)])


def swap_cores(array):
    count = lax.axis_size(BLOCKS)
    return lax.ppermute(array, BLOCKS, [(i, i ^ 1) for i in range(count)])


def body(queries, keys, values, grad_out, slot_pos, counts, seg_id):
    core = lax.axis_index(BLOCKS) % 2
    packed = pack(keys, values, slot_pos, counts, seg_id)
    across = shift_across(packed, 2)
    other = exchange(packed)
    behind = shift_blocks(packed, 2)
    *turned, own = turn(queries, grad_out, packed, packed)
    late = swap_cores(jnp.where(core == 0, other, behind))
    early = swap_cores(jnp.where(core == 0, own, across))
    pieces = (own, other, early, late, across, behind)
    attended, dscores, near_probs, middle, far, keys = attention(*turned, pieces)
    back = swap_cores(middle)
    near = near_gradients(turned[2], turned[3], dscores, near_probs)
    back = back.astype(F32)
    far = (far + jnp.where(core == 0, 0.0, back)).astype(BF16)
    near = near + jnp.where(core == 0, back, 0.0)
    far, dscores = lax.optimization_barrier((far, dscores))
    from_ahead = shift_blocks(far[1], -2)
    from_across = shift_across(far[0], -2)
    from_other = exchange(near[1].astype(BF16))
    grad_queries, attended = query_gradients(dscores, keys, attended)
    half = KEY_HEADS * HEAD
    totals = [
        (near[0][:, at] + from_across[:, at].astype(F32) + from_other[:, at].astype(F32) + from_ahead[:, at].astype(F32))
        .astype(BF16)[None]
        for at in (slice(0, half), slice(half, KV))
    ]
    return attended, grad_queries, totals[0], totals[1]


def solution(mesh):
    rows = P("grp", BLOCKS, None)
    slots = P("grp", BLOCKS)
    return jax.shard_map(
        body,
        mesh=mesh,
        in_specs=(rows, rows, rows, rows, slots, slots, P(BLOCKS)),
        out_specs=(rows, rows, rows, rows),
        check_vma=False,
    )
```
